32 devices in a mesh: row: 16 (over z, y, core), col: 2 (over x).
Axes of the slice: x: 2, y: 2, z: 4, core: 2. Of those that a mesh axis runs over, the one named last changes fastest.
Arguments:
- hamiltonian: float32 [3072, 3072], P('row', 'col'), may hold values from -2 to 2, as said below
- vectors: float32 [3072, 512], P(('row', 'col')), may hold values from -6 to 6
Outputs:
- filtered: float32 [3072, 512], P(('row', 'col'))
The draws below stay inside these ranges and needn't reach their ends.
Inputs may be any that keep to these rules, and one draw needn't show every extreme that they name: `hamiltonian`: exactly symmetric, with a diagonal part and a dense part of comparable weight.
All inputs are finite; a program needn't handle non-finite values.
Results may differ from the reference program's by a relative error of at most 0.0001.
Values sent between devices are 32-bit elements; how exact they have to be, the bound alone decides.
No kernel may reach another device: no remote copies, remote signals or barrier semaphores. Data moves between devices by JAX's collectives and lax.ppermute only.
A program may use at most 64 MiB of HBM per device.

```python
import jax
import jax.numpy as jnp
from jax import lax

NV = 512
DEGREE = 2
N = 3072


def draw_hamiltonian(key, part):
    base = jax.random.fold_in(key, 11)
    first, second = jax.random.split(base)
    dense = jnp.clip(jax.random.normal(first, (N, N), jnp.float32), -6.0, 6.0)
    diagonal = jax.random.uniform(second, (N,), jnp.float32, -1.0, 1.0)
    scale = 0.5 / jnp.sqrt(jnp.float32(N))
    return (dense + dense.T) * scale + jnp.diag(diagonal)


def shard_levels(own_key, dims, shards, smallest, high):
    factor_of = 1.0
    for dim, parts in shards:
        heights = jax.random.uniform(jax.random.fold_in(jax.random.fold_in(own_key, 6), dim), (parts,), jnp.float32, smallest / len(shards), high / len(shards))
        factor_of = factor_of * jnp.repeat(jnp.exp(heights), dims[dim] // parts).reshape((-1,) + (1,) * (len(dims) - 1 - dim))
    return factor_of


def gaussian(own_key, dims, scale, most, cuts=(), kind=jnp.bfloat16):
    result = scale * jax.random.normal(own_key, dims, jnp.float32)
    if cuts:
        result = result * shard_levels(own_key, dims, cuts, -0.22, 0.18)
    return jnp.clip(result, -most, most).astype(kind)


def setup_inputs(seed: int = 0) -> dict:
    splits = jax.random.split(jax.random.key(seed), 3)
    hamiltonian = draw_hamiltonian(jax.random.fold_in(splits[2], 71), 0)
    vectors = gaussian(splits[1], (N, NV), 1.0, 6.0, ((0, 32),), jnp.float32)
    return {"hamiltonian": hamiltonian, "vectors": vectors}


center = 0.6
half_width = 1.8


def reference(hamiltonian, vectors):
    def apply_shift(block):
        return jnp.dot(hamiltonian, block, precision=lax.Precision.HIGHEST, preferred_element_type=jnp.float32) - center * block

    older = vectors
    recent = vectors
    for degree in range(1, DEGREE + 1):
        product = apply_shift(recent)
        if degree == 1:
            fresh = product * (1.0 / half_width)
        else:
            fresh = (2.0 / half_width) * product - older
        older = recent
        recent = fresh
    return recent
```

```python
import jax
import jax.numpy as jnp
from jax import lax
from jax.sharding import PartitionSpec as P

DEGREE = 2
CHUNKS = 1

center = 0.6
half_width = 1.8


def product(left, right, left_dim):
    return lax.dot_general(
        left,
        right,
        (((left_dim,), (0,)), ((), ())),
        precision=lax.Precision.HIGH,
        preferred_element_type=jnp.float32,
    )


def on_device(rows, cols, hamiltonian, vectors):
    row_index = lax.axis_index("row")
    col_index = lax.axis_index("col")
    rows_block, cols_block = hamiltonian.shape
    part, width = vectors.shape
    half, quarter = width // 2, cols_block // 4
    core = row_index % 2
    place = (row_index // 2) % 4

    def exchange(block, row_mask, col_mask):
        mask = row_mask * cols + col_mask
        pairs = [(i, i ^ mask) for i in range(rows * cols)]
        return lax.ppermute(block, ("row", "col"), pairs)

    own_half = lax.dynamic_slice(vectors, (0, core * half), (part, half))
    other_half = lax.dynamic_slice(vectors, (0, (1 - core) * half), (part, half))
    pieces = []
    for k in range(cols):
        pieces.append(exchange(own_half, 0, k) if k else own_half)
        pieces.append(exchange(other_half, 1, k))
    block = jnp.concatenate(pieces, axis=0)

    global_rows = row_index * rows_block + lax.iota(jnp.int32, rows_block)
    global_cols = col_index * cols_block + lax.iota(jnp.int32, cols_block)
    on_diagonal = global_rows[:, None] == global_cols[None, :]
    shifted = hamiltonian - jnp.where(on_diagonal, jnp.float32(center), jnp.float32(0.0))
    shifted = jnp.concatenate(
        [lax.dynamic_slice(shifted, (0, (place ^ k) * quarter), (rows_block, quarter)) for k in (0, 2, 1, 3)], axis=1
    )
    mine = jnp.concatenate(
        [lax.dynamic_slice(shifted, ((col_index ^ k) * part, 0), (part, cols_block)) for k in range(cols)], axis=0
    )
    paired = exchange(mine, 1, 0)
    matrix = jnp.concatenate(
        [piece[k * part : (k + 1) * part] for k in range(cols) for piece in (mine, paired)], axis=0
    )
    kept, given = matrix[:, : 2 * quarter], matrix[:, 2 * quarter :]
    taken = exchange(given, 2, 0)
    square = jnp.concatenate([kept, taken], axis=0)

    span = half // CHUNKS
    chunks = [block[:, c * span : (c + 1) * span] for c in range(CHUNKS)]
    results = []
    for chunk in chunks:
        total = product(kept[:, :quarter], chunk, 0)
        others = [
            exchange(product(part_of, chunk, 0), 2 * k, 0)
            for k, part_of in ((3, given[:, quarter:]), (1, given[:, :quarter]), (2, kept[:, quarter:]))
        ]
        for term in others:
            total = total + term
        mask = 8
        while mask < rows:
            total = total + exchange(total, mask, 0)
            mask *= 2
        fresh = total * (1.0 / half_width)
        second = jnp.concatenate([fresh, exchange(fresh, 4, 0)], axis=0)
        partial = product(square, second, 1)
        total = partial[: 2 * part]
        terms = []
        for k in range(1, 2 * cols):
            terms.append(exchange(partial[2 * part * k : 2 * part * (k + 1)], 2 * (k // cols), k % cols))
        for term in terms:
            total = total + term
        results.append(total)
    total = jnp.concatenate(results, axis=1)
    own = total[:part]
    other = exchange(total[part:], 1, 0)
    first = jnp.where(core == 0, own, other)
    last = jnp.where(core == 0, other, own)
    return 2.0 / half_width * jnp.concatenate([first, last], axis=1) - vectors


def solution(mesh):
    rows, cols = mesh.shape["row"], mesh.shape["col"]

    def local(hamiltonian, vectors):
        return on_device(rows, cols, hamiltonian, vectors)

    return jax.shard_map(
        local,
        mesh=mesh,
        in_specs=(P("row", "col"), P(("row", "col"), None)),
        out_specs=P(("row", "col"), None),
        check_vma=False,
    )
```

```python
import jax
import jax.numpy as jnp
from jax import lax
from jax.sharding import PartitionSpec as P

DEGREE = 2
CHUNKS = 2

center = 0.6
half_width = 1.8


def product(left, right, left_dim):
    return lax.dot_general(
        left,
        right,
        (((left_dim,), (0,)), ((), ())),
        precision=lax.Precision.HIGH,
        preferred_element_type=jnp.float32,
    )


def after(value, *earlier):
    return lax.optimization_barrier((value, *earlier))[0]


def on_device(rows, cols, hamiltonian, vectors):
    row_index = lax.axis_index("row")
    col_index = lax.axis_index("col")
    rows_block, cols_block = hamiltonian.shape
    part, width = vectors.shape
    half, quarter = width // 2, cols_block // 4
    span = half // CHUNKS
    core = row_index % 2
    place = (row_index // 2) % 4

    def exchange(block, row_masks, col_mask):
        masks = row_masks if isinstance(row_masks, tuple) else (row_masks, row_masks)
        pairs = [(i, i ^ (masks[i // cols % 2] * cols + col_mask)) for i in range(rows * cols)]
        return lax.ppermute(block, ("row", "col"), pairs)

    partner = exchange(hamiltonian, 1, 0)
    order = [place, place ^ (2 - core), place ^ (1 + core), place ^ 3]

    def prepared(block, block_row):
        global_rows = block_row * rows_block + lax.iota(jnp.int32, rows_block)
        global_cols = col_index * cols_block + lax.iota(jnp.int32, cols_block)
        on_diagonal = global_rows[:, None] == global_cols[None, :]
        shifted = block - jnp.where(on_diagonal, jnp.float32(center), jnp.float32(0.0))
        placed = jnp.concatenate(
            [lax.dynamic_slice(shifted, (0, q * quarter), (rows_block, quarter)) for q in order], axis=1
        )
        return [lax.dynamic_slice(placed, ((col_index ^ k) * part, 0), (part, cols_block)) for k in range(cols)]

    ours, theirs = prepared(hamiltonian, row_index), prepared(partner, row_index ^ 1)
    matrix = jnp.concatenate([block for k in range(cols) for block in (ours[k], theirs[k])], axis=0)

    chunks = []
    for c in range(CHUNKS):
        own = lax.dynamic_slice(vectors, (0, core * half + c * span), (part, span))
        other = lax.dynamic_slice(vectors, (0, (1 - core) * half + c * span), (part, span))
        if c:
            own, other, _ = lax.optimization_barrier((own, other, matrix))
        pieces = []
        for k in range(cols):
            pieces.append(exchange(own, 0, k) if k else own)
            pieces.append(exchange(other, 1, k))
        chunks.append(jnp.concatenate(pieces, axis=0))

    results = []
    given = partial = None
    for chunk in chunks:
        if results:
            chunk = after(chunk, given)
        given = product(matrix[:, 2 * quarter :], chunk, 0)
        received = exchange(given, (2, 4), 0)
        passed = product(matrix[:, quarter : 2 * quarter], chunk, 0) + received[quarter:]
        total = product(matrix[:, :quarter], chunk, 0) + received[:quarter]
        total = total + exchange(passed, (4, 2), 0)
        mask = 8
        while mask < rows:
            total = total + exchange(total, mask, 0)
            mask *= 2
        fresh = total * (1.0 / half_width)
        fresh = jnp.concatenate([fresh, exchange(fresh, (4, 2), 0)], axis=0)
        fresh = jnp.concatenate([fresh, exchange(fresh, (2, 4), 0)], axis=0)
        if results:
            fresh = after(fresh, partial)
        partial = product(matrix, fresh, 1)
        total = partial[: 2 * part]
        for term in [exchange(partial[2 * part * k : 2 * part * (k + 1)], 0, k) for k in range(1, cols)]:
            total = total + term
        results.append(total)
    total = jnp.concatenate(results, axis=1)
    own = total[:part]
    other = exchange(total[part:], 1, 0)
    first = jnp.where(core == 0, own, other)
    last = jnp.where(core == 0, other, own)
    return 2.0 / half_width * jnp.concatenate([first, last], axis=1) - vectors


def solution(mesh):
    rows, cols = mesh.shape["row"], mesh.shape["col"]

    def local(hamiltonian, vectors):
        return on_device(rows, cols, hamiltonian, vectors)

    return jax.shard_map(
        local,
        mesh=mesh,
        in_specs=(P("row", "col"), P(("row", "col"), None)),
        out_specs=P(("row", "col"), None),
        check_vma=False,
    )
```

```python
import jax
import jax.numpy as jnp
from jax import lax
from jax.sharding import PartitionSpec as P

DEGREE = 2
CHUNKS = 2

center = 0.6
half_width = 1.8


def product(left, right, left_dim):
    return lax.dot_general(
        left,
        right,
        (((left_dim,), (0,)), ((), ())),
        precision=lax.Precision.HIGH,
        preferred_element_type=jnp.float32,
    )


def after(value, *earlier):
    return lax.optimization_barrier((value, *earlier))[0]


def on_device(rows, cols, hamiltonian, vectors):
    row_index = lax.axis_index("row")
    col_index = lax.axis_index("col")
    rows_block, cols_block = hamiltonian.shape
    part, width = vectors.shape
    half, quarter = width // 2, cols_block // 4
    span = half // CHUNKS
    core = row_index % 2
    place = (row_index // 2) % 4

    def exchange(block, row_masks, col_mask):
        masks = row_masks if isinstance(row_masks, tuple) else (row_masks, row_masks)
        pairs = [(i, i ^ (masks[i // cols % 2] * cols + col_mask)) for i in range(rows * cols)]
        return lax.ppermute(block, ("row", "col"), pairs)

    partner = exchange(hamiltonian, 1, 0)
    order = [place, place ^ (2 - core), place ^ (1 + core), place ^ 3]

    def prepared(block, block_row):
        global_rows = block_row * rows_block + lax.iota(jnp.int32, rows_block)
        global_cols = col_index * cols_block + lax.iota(jnp.int32, cols_block)
        on_diagonal = global_rows[:, None] == global_cols[None, :]
        shifted = block - jnp.where(on_diagonal, jnp.float32(center), jnp.float32(0.0))
        placed = jnp.concatenate(
            [lax.dynamic_slice(shifted, (0, q * quarter), (rows_block, quarter)) for q in order], axis=1
        )
        return [lax.dynamic_slice(placed, ((col_index ^ k) * part, 0), (part, cols_block)) for k in range(cols)]

    ours, theirs = prepared(hamiltonian, row_index), prepared(partner, row_index ^ 1)
    matrix = jnp.concatenate([block for k in range(cols) for block in (ours[k], theirs[k])], axis=0)

    chunks = []
    for c in range(CHUNKS):
        own = lax.dynamic_slice(vectors, (0, core * half + c * span), (part, span))
        other = lax.dynamic_slice(vectors, (0, (1 - core) * half + c * span), (part, span))
        if c:
            own, other, _ = lax.optimization_barrier((own, other, matrix))
        pieces = []
        for k in range(cols):
            pieces.append(exchange(own, 0, k) if k else own)
            pieces.append(exchange(other, 1, k))
        chunks.append(jnp.concatenate(pieces, axis=0))

    results = []
    given = partial = None
    for chunk in chunks:
        if results:
            chunk = after(chunk, given)
        given = product(matrix[:, quarter:], chunk, 0)
        sent = [given[i * quarter : (i + 1) * quarter] for i in (1, 0, 2)]
        MASKS = [((4, 2), (2, 4), (6, 6))[i] for i in (1, 0, 2)]
        received = [exchange(block, masks, 0) for block, masks in zip(sent, MASKS)]
        total = product(matrix[:, :quarter], chunk, 0)
        for term in received:
            total = total + term
        mask = 8
        while mask < rows:
            total = total + exchange(total, mask, 0)
            mask *= 2
        fresh = total * (1.0 / half_width)
        fresh = jnp.concatenate([fresh, *[exchange(fresh, masks, 0) for masks in ((4, 2), (2, 4), (6, 6))]], axis=0)
        if results:
            fresh = after(fresh, partial)
        partial = product(matrix, fresh, 1)
        total = partial[: 2 * part]
        for term in [exchange(partial[2 * part * k : 2 * part * (k + 1)], 0, k) for k in range(1, cols)]:
            total = total + term
        results.append(total)
    total = jnp.concatenate(results, axis=1)
    own = total[:part]
    other = exchange(total[part:], 1, 0)
    first = jnp.where(core == 0, own, other)
    last = jnp.where(core == 0, other, own)
    return 2.0 / half_width * jnp.concatenate([first, last], axis=1) - vectors


def solution(mesh):
    rows, cols = mesh.shape["row"], mesh.shape["col"]

    def local(hamiltonian, vectors):
        return on_device(rows, cols, hamiltonian, vectors)

    return jax.shard_map(
        local,
        mesh=mesh,
        in_specs=(P("row", "col"), P(("row", "col"), None)),
        out_specs=P(("row", "col"), None),
        check_vma=False,
    )
```

```python
import jax
import jax.numpy as jnp
from jax import lax
from jax.sharding import PartitionSpec as P

DEGREE = 2
CHUNKS = 2

center = 0.6
half_width = 1.8


def product(left, right, left_dim):
    return lax.dot_general(
        left,
        right,
        (((left_dim,), (0,)), ((), ())),
        precision=lax.Precision.HIGH,
        preferred_element_type=jnp.float32,
    )


def after(value, *earlier):
    return lax.optimization_barrier((value, *earlier))[0]


def on_device(rows, cols, hamiltonian, vectors):
    row_index = lax.axis_index("row")
    col_index = lax.axis_index("col")
    rows_block, cols_block = hamiltonian.shape
    part, width = vectors.shape
    half, quarter = width // 2, cols_block // 4
    span = half // CHUNKS
    core = row_index % 2
    place = (row_index // 2) % 4

    def exchange(block, row_masks, col_mask):
        masks = row_masks if isinstance(row_masks, tuple) else (row_masks, row_masks)
        pairs = [(i, i ^ (masks[i // cols % 2] * cols + col_mask)) for i in range(rows * cols)]
        return lax.ppermute(block, ("row", "col"), pairs)

    partner = exchange(hamiltonian, 1, 0)
    order = [place, place ^ (2 - core), place ^ (1 + core), place ^ 3]

    def prepared(block, block_row):
        global_rows = block_row * rows_block + lax.iota(jnp.int32, rows_block)
        global_cols = col_index * cols_block + lax.iota(jnp.int32, cols_block)
        on_diagonal = global_rows[:, None] == global_cols[None, :]
        shifted = block - jnp.where(on_diagonal, jnp.float32(center), jnp.float32(0.0))
        placed = jnp.concatenate(
            [lax.dynamic_slice(shifted, (0, q * quarter), (rows_block, quarter)) for q in order], axis=1
        )
        return [lax.dynamic_slice(placed, ((col_index ^ k) * part, 0), (part, cols_block)) for k in range(cols)]

    ours, theirs = prepared(hamiltonian, row_index), prepared(partner, row_index ^ 1)
    matrix = jnp.concatenate([block for k in range(cols) for block in (ours[k], theirs[k])], axis=0)

    chunks = []
    for c in range(CHUNKS):
        own = lax.dynamic_slice(vectors, (0, core * half + c * span), (part, span))
        other = lax.dynamic_slice(vectors, (0, (1 - core) * half + c * span), (part, span))
        if c:
            own, other, _ = lax.optimization_barrier((own, other, matrix))
        pieces = []
        for k in range(cols):
            pieces.append(exchange(own, 0, k) if k else own)
            pieces.append(exchange(other, 1, k))
        chunks.append(jnp.concatenate(pieces, axis=0))

    def together(terms):
        return lax.optimization_barrier(tuple(terms))

    partners = ((2, 4), (4, 2), (6, 6))
    quarters = (2, 1, 3)
    sums = []
    given = None
    for chunk in chunks:
        if sums:
            chunk = after(chunk, given)
        given = product(matrix[:, quarter:], chunk, 0)
        sent = [given[(i - 1) * quarter : i * quarter] for i in quarters]
        received = together([exchange(block, masks, 0) for block, masks in zip(sent, partners)])
        total = product(matrix[:, :quarter], chunk, 0)
        for term in received:
            total = total + term
        sums.append(total)

    partials = []
    for total in sums:
        mask = 8
        while mask < rows:
            total = total + exchange(total, mask, 0)
            mask *= 2
        fresh = total * (1.0 / half_width)
        received = dict(zip(quarters, [exchange(fresh, masks, 0) for masks in partners]))
        fresh = jnp.concatenate([fresh, received[1], received[2], received[3]], axis=0)
        if partials:
            fresh = after(fresh, partials[-1])
        partials.append(product(matrix, fresh, 1))

    owns, others, lasts = [], [], []
    for partial in partials[:-1]:
        total = partial[: 2 * part]
        for term in [exchange(partial[2 * part * k : 2 * part * (k + 1)], 0, k) for k in range(1, cols)]:
            total = total + term
        owns.append(total[:part])
        lasts.append(total[part:])
    partial = partials[-1]
    moves = [(k, c) for k in range(cols) for c in range(2)][1:]
    terms = together(
        [exchange(partial[(2 * k + c) * part : (2 * k + c + 1) * part], c, k) for k, c in moves]
    )
    own, other = partial[:part], None
    for (_, c), term in zip(moves, terms):
        if c == 0:
            own = own + term
        else:
            other = term if other is None else other + term
    own = jnp.concatenate([*owns, own], axis=1)
    others = [exchange(last, 1, 0) for last in lasts]
    other = jnp.concatenate([*others, other], axis=1)
    first = jnp.where(core == 0, own, other)
    last = jnp.where(core == 0, other, own)
    return 2.0 / half_width * jnp.concatenate([first, last], axis=1) - vectors


def solution(mesh):
    rows, cols = mesh.shape["row"], mesh.shape["col"]

    def local(hamiltonian, vectors):
        return on_device(rows, cols, hamiltonian, vectors)

    return jax.shard_map(
        local,
        mesh=mesh,
        in_specs=(P("row", "col"), P(("row", "col"), None)),
        out_specs=P(("row", "col"), None),
        check_vma=False,
    )
```

```python
import jax
import jax.numpy as jnp
from jax import lax
from jax.sharding import PartitionSpec as P

DEGREE = 2
CHUNKS = 2

center = 0.6
half_width = 1.8


def product(left, right, left_dim):
    return lax.dot_general(
        left,
        right,
        (((left_dim,), (0,)), ((), ())),
        precision=lax.Precision.HIGH,
        preferred_element_type=jnp.float32,
    )


def after(value, *earlier):
    return lax.optimization_barrier((value, *earlier))[0]


def on_device(rows, cols, hamiltonian, vectors):
    row_index = lax.axis_index("row")
    col_index = lax.axis_index("col")
    rows_block, cols_block = hamiltonian.shape
    part, width = vectors.shape
    half, quarter = width // 2, cols_block // 4
    span = half // CHUNKS
    core = row_index % 2
    place = (row_index // 2) % 4

    def exchange(block, row_masks, col_mask):
        masks = row_masks if isinstance(row_masks, tuple) else (row_masks, row_masks)
        pairs = [(i, i ^ (masks[i // cols % 2] * cols + col_mask)) for i in range(rows * cols)]
        return lax.ppermute(block, ("row", "col"), pairs)

    partner = exchange(hamiltonian, 1, 0)
    order = [place, place ^ (2 - core), place ^ (1 + core), place ^ 3]

    def prepared(block, block_row):
        global_rows = block_row * rows_block + lax.iota(jnp.int32, rows_block)
        global_cols = col_index * cols_block + lax.iota(jnp.int32, cols_block)
        on_diagonal = global_rows[:, None] == global_cols[None, :]
        shifted = block - jnp.where(on_diagonal, jnp.float32(center), jnp.float32(0.0))
        placed = jnp.concatenate(
            [lax.dynamic_slice(shifted, (0, q * quarter), (rows_block, quarter)) for q in order], axis=1
        )
        return [lax.dynamic_slice(placed, ((col_index ^ k) * part, 0), (part, cols_block)) for k in range(cols)]

    ours, theirs = prepared(hamiltonian, row_index), prepared(partner, row_index ^ 1)
    matrix = jnp.concatenate([block for k in range(cols) for block in (ours[k], theirs[k])], axis=0)

    chunks = []
    for c in range(CHUNKS):
        own = lax.dynamic_slice(vectors, (0, core * half + c * span), (part, span))
        other = lax.dynamic_slice(vectors, (0, (1 - core) * half + c * span), (part, span))
        if c:
            own, other, _ = lax.optimization_barrier((own, other, matrix))
        pieces = []
        for k in range(cols):
            pieces.append(exchange(own, 0, k) if k else own)
            pieces.append(exchange(other, 1, k))
        chunks.append(jnp.concatenate(pieces, axis=0))

    def together(terms):
        return lax.optimization_barrier(tuple(terms))

    partners = ((2, 4), (4, 2), (6, 6))
    quarters = (2, 1, 3)
    sums = []
    given = None
    for chunk in chunks:
        if sums:
            chunk = after(chunk, given)
            given = product(matrix[:, 2 * quarter :], chunk, 0)
            crossed = exchange(given[quarter:], partners[0], 0)
            straight = exchange(given[:quarter], partners[0], 0)
            passed = product(matrix[:, quarter : 2 * quarter], chunk, 0) + crossed
            total = product(matrix[:, :quarter], chunk, 0) + straight + exchange(passed, partners[1], 0)
        else:
            given = product(matrix[:, quarter:], chunk, 0)
            sent = [given[(i - 1) * quarter : i * quarter] for i in quarters]
            received = together([exchange(block, masks, 0) for block, masks in zip(sent, partners)])
            total = product(matrix[:, :quarter], chunk, 0)
            for term in received:
                total = total + term
        sums.append(total)

    partials = []
    for total in sums:
        mask = 8
        while mask < rows:
            total = total + exchange(total, mask, 0)
            mask *= 2
        fresh = total * (1.0 / half_width)
        if partials:
            received = dict(zip(quarters, [exchange(fresh, masks, 0) for masks in partners]))
            fresh = jnp.concatenate([fresh, received[1], received[2], received[3]], axis=0)
            fresh = after(fresh, partials[-1])
        else:
            second, first = together([exchange(fresh, partners[1], 0), exchange(fresh, partners[0], 0)])
            fresh = jnp.concatenate([fresh, second, first, exchange(second, partners[0], 0)], axis=0)
        partials.append(product(matrix, fresh, 1))

    owns, others, lasts = [], [], []
    for partial in partials[:-1]:
        total = partial[: 2 * part]
        for term in [exchange(partial[2 * part * k : 2 * part * (k + 1)], 0, k) for k in range(1, cols)]:
            total = total + term
        owns.append(total[:part])
        lasts.append(total[part:])
    partial = partials[-1]
    moves = [(k, c) for k in range(cols) for c in range(2)][1:]
    terms = together(
        [exchange(partial[(2 * k + c) * part : (2 * k + c + 1) * part], c, k) for k, c in moves]
    )
    own, other = partial[:part], None
    for (_, c), term in zip(moves, terms):
        if c == 0:
            own = own + term
        else:
            other = term if other is None else other + term
    own = jnp.concatenate([*owns, own], axis=1)
    others = [exchange(last, 1, 0) for last in lasts]
    other = jnp.concatenate([*others, other], axis=1)
    first = jnp.where(core == 0, own, other)
    last = jnp.where(core == 0, other, own)
    return 2.0 / half_width * jnp.concatenate([first, last], axis=1) - vectors


def solution(mesh):
    rows, cols = mesh.shape["row"], mesh.shape["col"]

    def local(hamiltonian, vectors):
        return on_device(rows, cols, hamiltonian, vectors)

    return jax.shard_map(
        local,
        mesh=mesh,
        in_specs=(P("row", "col"), P(("row", "col"), None)),
        out_specs=P(("row", "col"), None),
        check_vma=False,
    )
```

```python
import jax
import jax.numpy as jnp
from jax import lax
from jax.sharding import PartitionSpec as P

DEGREE = 2
CHUNKS = 2

center = 0.6
half_width = 1.8


def product(left, right, left_dim):
    return lax.dot_general(
        left,
        right,
        (((left_dim,), (0,)), ((), ())),
        precision=lax.Precision.HIGH,
        preferred_element_type=jnp.float32,
    )


def after(value, *earlier):
    return lax.optimization_barrier((value, *earlier))[0]


def on_device(rows, cols, hamiltonian, vectors):
    row_index = lax.axis_index("row")
    col_index = lax.axis_index("col")
    rows_block, cols_block = hamiltonian.shape
    part, width = vectors.shape
    half, quarter = width // 2, cols_block // 4
    span = half // CHUNKS
    core = row_index % 2
    place = (row_index // 2) % 4

    def exchange(block, row_masks, col_mask):
        masks = row_masks if isinstance(row_masks, tuple) else (row_masks, row_masks)
        pairs = [(i, i ^ (masks[i // cols % 2] * cols + col_mask)) for i in range(rows * cols)]
        return lax.ppermute(block, ("row", "col"), pairs)

    partner = exchange(hamiltonian, 1, 0)
    order = [place, place ^ (2 - core), place ^ (1 + core), place ^ 3]

    def prepared(block, block_row):
        global_rows = block_row * rows_block + lax.iota(jnp.int32, rows_block)
        global_cols = col_index * cols_block + lax.iota(jnp.int32, cols_block)
        on_diagonal = global_rows[:, None] == global_cols[None, :]
        shifted = block - jnp.where(on_diagonal, jnp.float32(center), jnp.float32(0.0))
        placed = jnp.concatenate(
            [lax.dynamic_slice(shifted, (0, q * quarter), (rows_block, quarter)) for q in order], axis=1
        )
        return [lax.dynamic_slice(placed, ((col_index ^ k) * part, 0), (part, cols_block)) for k in range(cols)]

    ours, theirs = prepared(hamiltonian, row_index), prepared(partner, row_index ^ 1)
    matrix = jnp.concatenate([block for k in range(cols) for block in (ours[k], theirs[k])], axis=0)

    chunks = []
    for c in range(CHUNKS):
        own = lax.dynamic_slice(vectors, (0, core * half + c * span), (part, span))
        other = lax.dynamic_slice(vectors, (0, (1 - core) * half + c * span), (part, span))
        if c:
            own, other, _ = lax.optimization_barrier((own, other, matrix))
        pieces = []
        for k in range(cols):
            pieces.append(exchange(own, 0, k) if k else own)
            pieces.append(exchange(other, 1, k))
        chunks.append(jnp.concatenate(pieces, axis=0))

    def together(terms):
        return lax.optimization_barrier(tuple(terms))

    partners = ((2, 4), (4, 2), (6, 6))
    quarters = (2, 1, 3)
    sums = []
    given = None
    for chunk in chunks:
        if sums:
            chunk = after(chunk, given)
            given = product(matrix[:, 2 * quarter :], chunk, 0)
            crossed = exchange(given[quarter:], partners[0], 0)
            straight = exchange(given[:quarter], partners[0], 0)
            passed = product(matrix[:, quarter : 2 * quarter], chunk, 0) + crossed
            total = product(matrix[:, :quarter], chunk, 0) + straight + exchange(passed, partners[1], 0)
        else:
            given = product(matrix[:, quarter:], chunk, 0)
            sent = [given[(i - 1) * quarter : i * quarter] for i in quarters]
            received = together([exchange(block, masks, 0) for block, masks in zip(sent, partners)])
            total = product(matrix[:, :quarter], chunk, 0)
            for term in received:
                total = total + term
        sums.append(total)

    partials = []
    for total in sums:
        mask = 8
        while mask < rows:
            total = total + exchange(total, mask, 0)
            mask *= 2
        fresh = total * (1.0 / half_width)
        if partials:
            received = dict(zip(quarters, together([exchange(fresh, masks, 0) for masks in partners])))
            fresh = jnp.concatenate([fresh, received[1], received[2], received[3]], axis=0)
            fresh = after(fresh, partials[-1])
        else:
            second, first = together([exchange(fresh, partners[1], 0), exchange(fresh, partners[0], 0)])
            fresh = jnp.concatenate([fresh, second, first, exchange(second, partners[0], 0)], axis=0)
        partials.append(product(matrix, fresh, 1))

    owns, others, lasts = [], [], []
    for partial in partials[:-1]:
        total = partial[: 2 * part]
        for term in [exchange(partial[2 * part * k : 2 * part * (k + 1)], 0, k) for k in range(1, cols)]:
            total = total + term
        owns.append(total[:part])
        lasts.append(total[part:])
    partial = partials[-1]
    moves = [(k, c) for k in range(cols) for c in range(2)][1:]
    terms = together(
        [exchange(partial[(2 * k + c) * part : (2 * k + c + 1) * part], c, k) for k, c in moves]
    )
    own, other = partial[:part], None
    for (_, c), term in zip(moves, terms):
        if c == 0:
            own = own + term
        else:
            other = term if other is None else other + term
    own = jnp.concatenate([*owns, own], axis=1)
    others = [exchange(last, 1, 0) for last in lasts]
    other = jnp.concatenate([*others, other], axis=1)
    first = jnp.where(core == 0, own, other)
    last = jnp.where(core == 0, other, own)
    return 2.0 / half_width * jnp.concatenate([first, last], axis=1) - vectors


def solution(mesh):
    rows, cols = mesh.shape["row"], mesh.shape["col"]

    def local(hamiltonian, vectors):
        return on_device(rows, cols, hamiltonian, vectors)

    return jax.shard_map(
        local,
        mesh=mesh,
        in_specs=(P("row", "col"), P(("row", "col"), None)),
        out_specs=P(("row", "col"), None),
        check_vma=False,
    )
```

```python
import jax
import jax.numpy as jnp
from jax import lax
from jax.sharding import PartitionSpec as P

DEGREE = 2
CHUNKS = 2

center = 0.6
half_width = 1.8


def product(left, right, left_dim):
    return lax.dot_general(
        left,
        right,
        (((left_dim,), (0,)), ((), ())),
        precision=lax.Precision.HIGH,
        preferred_element_type=jnp.float32,
    )


def after(value, *earlier):
    return lax.optimization_barrier((value, *earlier))[0]


def on_device(rows, cols, hamiltonian, vectors):
    row_index = lax.axis_index("row")
    col_index = lax.axis_index("col")
    rows_block, cols_block = hamiltonian.shape
    part, width = vectors.shape
    half, quarter = width // 2, cols_block // 4
    span = half // CHUNKS
    core = row_index % 2
    place = (row_index // 2) % 4

    def exchange(block, row_masks, col_mask):
        masks = row_masks if isinstance(row_masks, tuple) else (row_masks, row_masks)
        pairs = [(i, i ^ (masks[i // cols % 2] * cols + col_mask)) for i in range(rows * cols)]
        return lax.ppermute(block, ("row", "col"), pairs)

    partner = exchange(hamiltonian, 1, 0)
    order = [place, place ^ (2 - core), place ^ (1 + core), place ^ 3]

    def prepared(block, block_row):
        global_rows = block_row * rows_block + lax.iota(jnp.int32, rows_block)
        global_cols = col_index * cols_block + lax.iota(jnp.int32, cols_block)
        on_diagonal = global_rows[:, None] == global_cols[None, :]
        shifted = block - jnp.where(on_diagonal, jnp.float32(center), jnp.float32(0.0))
        placed = jnp.concatenate(
            [lax.dynamic_slice(shifted, (0, q * quarter), (rows_block, quarter)) for q in order], axis=1
        )
        return [lax.dynamic_slice(placed, ((col_index ^ k) * part, 0), (part, cols_block)) for k in range(cols)]

    ours, theirs = prepared(hamiltonian, row_index), prepared(partner, row_index ^ 1)
    matrix = jnp.concatenate([block for k in range(cols) for block in (ours[k], theirs[k])], axis=0)

    chunks = []
    for c in range(CHUNKS):
        own = lax.dynamic_slice(vectors, (0, core * half + c * span), (part, span))
        other = lax.dynamic_slice(vectors, (0, (1 - core) * half + c * span), (part, span))
        if c:
            own, other, _ = lax.optimization_barrier((own, other, matrix))
        pieces = []
        for k in range(cols):
            pieces.append(exchange(own, 0, k) if k else own)
            pieces.append(exchange(other, 1, k))
        chunks.append(jnp.concatenate(pieces, axis=0))

    def together(terms):
        return lax.optimization_barrier(tuple(terms))

    partners = ((2, 4), (4, 2), (6, 6))
    quarters = (2, 1, 3)
    sums = []
    given = None
    for chunk in chunks:
        if sums:
            chunk = after(chunk, given)
            given = product(matrix[:, 2 * quarter :], chunk, 0)
            crossed = exchange(given[quarter:], partners[0], 0)
            straight = exchange(given[:quarter], partners[0], 0)
            passed = product(matrix[:, quarter : 2 * quarter], chunk, 0) + crossed
            straight, passed = together([straight, exchange(passed, partners[1], 0)])
            total = product(matrix[:, :quarter], chunk, 0) + straight + passed
        else:
            given = product(matrix[:, quarter:], chunk, 0)
            sent = [given[(i - 1) * quarter : i * quarter] for i in quarters]
            received = together([exchange(block, masks, 0) for block, masks in zip(sent, partners)])
            total = product(matrix[:, :quarter], chunk, 0)
            for term in received:
                total = total + term
        sums.append(total)

    partials = []
    for total in sums:
        mask = 8
        while mask < rows:
            total = total + exchange(total, mask, 0)
            mask *= 2
        fresh = total * (1.0 / half_width)
        if partials:
            received = dict(zip(quarters, together([exchange(fresh, masks, 0) for masks in partners])))
            fresh = jnp.concatenate([fresh, received[1], received[2], received[3]], axis=0)
            fresh = after(fresh, partials[-1])
        else:
            second, first = together([exchange(fresh, partners[1], 0), exchange(fresh, partners[0], 0)])
            fresh = jnp.concatenate([fresh, second, first, exchange(second, partners[0], 0)], axis=0)
        partials.append(product(matrix, fresh, 1))

    owns, others, lasts = [], [], []
    for partial in partials[:-1]:
        total = partial[: 2 * part]
        for term in [exchange(partial[2 * part * k : 2 * part * (k + 1)], 0, k) for k in range(1, cols)]:
            total = total + term
        owns.append(total[:part])
        lasts.append(total[part:])
    partial = partials[-1]
    moves = [(k, c) for k in range(cols) for c in range(2)][1:]
    terms = together(
        [exchange(partial[(2 * k + c) * part : (2 * k + c + 1) * part], c, k) for k, c in moves]
    )
    own, other = partial[:part], None
    for (_, c), term in zip(moves, terms):
        if c == 0:
            own = own + term
        else:
            other = term if other is None else other + term
    own = jnp.concatenate([*owns, own], axis=1)
    others = [exchange(last, 1, 0) for last in lasts]
    other = jnp.concatenate([*others, other], axis=1)
    first = jnp.where(core == 0, own, other)
    last = jnp.where(core == 0, other, own)
    return 2.0 / half_width * jnp.concatenate([first, last], axis=1) - vectors


def solution(mesh):
    rows, cols = mesh.shape["row"], mesh.shape["col"]

    def local(hamiltonian, vectors):
        return on_device(rows, cols, hamiltonian, vectors)

    return jax.shard_map(
        local,
        mesh=mesh,
        in_specs=(P("row", "col"), P(("row", "col"), None)),
        out_specs=P(("row", "col"), None),
        check_vma=False,
    )
```

```python
import jax
import jax.numpy as jnp
from jax import lax
from jax.sharding import PartitionSpec as P

DEGREE = 2
CHUNKS = 2

center = 0.6
half_width = 1.8


def product(left, right, left_dim):
    return lax.dot_general(
        left,
        right,
        (((left_dim,), (0,)), ((), ())),
        precision=lax.Precision.HIGH,
        preferred_element_type=jnp.float32,
    )


def after(value, *earlier):
    return lax.optimization_barrier((value, *earlier))[0]


def on_device(rows, cols, hamiltonian, vectors):
    row_index = lax.axis_index("row")
    col_index = lax.axis_index("col")
    rows_block, cols_block = hamiltonian.shape
    part, width = vectors.shape
    half, quarter = width // 2, cols_block // 4
    span = half // CHUNKS
    core = row_index % 2
    place = (row_index // 2) % 4

    def exchange(block, row_masks, col_mask):
        masks = row_masks if isinstance(row_masks, tuple) else (row_masks, row_masks)
        pairs = [(i, i ^ (masks[i // cols % 2] * cols + col_mask)) for i in range(rows * cols)]
        return lax.ppermute(block, ("row", "col"), pairs)

    partner = exchange(hamiltonian, 1, 0)
    order = [place, place ^ (2 - core), place ^ (1 + core), place ^ 3]

    def prepared(block, block_row):
        global_rows = block_row * rows_block + lax.iota(jnp.int32, rows_block)
        global_cols = col_index * cols_block + lax.iota(jnp.int32, cols_block)
        on_diagonal = global_rows[:, None] == global_cols[None, :]
        shifted = block - jnp.where(on_diagonal, jnp.float32(center), jnp.float32(0.0))
        placed = jnp.concatenate(
            [lax.dynamic_slice(shifted, (0, q * quarter), (rows_block, quarter)) for q in order], axis=1
        )
        return [lax.dynamic_slice(placed, ((col_index ^ k) * part, 0), (part, cols_block)) for k in range(cols)]

    ours, theirs = prepared(hamiltonian, row_index), prepared(partner, row_index ^ 1)
    matrix = jnp.concatenate([block for k in range(cols) for block in (ours[k], theirs[k])], axis=0)

    chunks = []
    for c in range(CHUNKS):
        own = lax.dynamic_slice(vectors, (0, core * half + c * span), (part, span))
        other = lax.dynamic_slice(vectors, (0, (1 - core) * half + c * span), (part, span))
        if c:
            own, other, _ = lax.optimization_barrier((own, other, matrix))
        pieces = []
        for k in range(cols):
            pieces.append(exchange(own, 0, k) if k else own)
            pieces.append(exchange(other, 1, k))
        chunks.append(jnp.concatenate(pieces, axis=0))

    def together(terms):
        return lax.optimization_barrier(tuple(terms))

    partners = ((2, 4), (4, 2), (6, 6))
    quarters = (2, 1, 3)
    sums = []
    given = None
    for chunk in chunks:
        if sums:
            chunk = after(chunk, given)
            given = product(matrix[:, 2 * quarter :], chunk, 0)
            crossed = exchange(given[quarter:], partners[0], 0)
            straight = exchange(given[:quarter], partners[0], 0)
            passed = product(matrix[:, quarter : 2 * quarter], chunk, 0) + crossed
            total = product(matrix[:, :quarter], chunk, 0) + straight + exchange(passed, partners[1], 0)
        else:
            given = product(matrix[:, quarter:], chunk, 0)
            sent = [given[(i - 1) * quarter : i * quarter] for i in quarters]
            received = together([exchange(block, masks, 0) for block, masks in zip(sent, partners)])
            total = product(matrix[:, :quarter], chunk, 0)
            for term in received:
                total = total + term
        sums.append(total)

    partials = []
    for total in sums:
        mask = 8
        while mask < rows:
            total = total + exchange(total, mask, 0)
            mask *= 2
        fresh = total * (1.0 / half_width)
        if partials:
            received = dict(zip(quarters, together([exchange(fresh, masks, 0) for masks in partners])))
            fresh = jnp.concatenate([fresh, received[1], received[2], received[3]], axis=0)
        else:
            second, first = together([exchange(fresh, partners[1], 0), exchange(fresh, partners[0], 0)])
            fresh = jnp.concatenate([fresh, second, first, exchange(second, partners[0], 0)], axis=0)
        partials.append(product(matrix, fresh, 1))

    owns, others, lasts = [], [], []
    for partial in partials[:-1]:
        total = partial[: 2 * part]
        for term in [exchange(partial[2 * part * k : 2 * part * (k + 1)], 0, k) for k in range(1, cols)]:
            total = total + term
        owns.append(total[:part])
        lasts.append(total[part:])
    partial = partials[-1]
    moves = [(k, c) for k in range(cols) for c in range(2)][1:]
    terms = together(
        [exchange(partial[(2 * k + c) * part : (2 * k + c + 1) * part], c, k) for k, c in moves]
    )
    own, other = partial[:part], None
    for (_, c), term in zip(moves, terms):
        if c == 0:
            own = own + term
        else:
            other = term if other is None else other + term
    own = jnp.concatenate([*owns, own], axis=1)
    others = [exchange(last, 1, 0) for last in lasts]
    other = jnp.concatenate([*others, other], axis=1)
    first = jnp.where(core == 0, own, other)
    last = jnp.where(core == 0, other, own)
    return 2.0 / half_width * jnp.concatenate([first, last], axis=1) - vectors


def solution(mesh):
    rows, cols = mesh.shape["row"], mesh.shape["col"]

    def local(hamiltonian, vectors):
        return on_device(rows, cols, hamiltonian, vectors)

    return jax.shard_map(
        local,
        mesh=mesh,
        in_specs=(P("row", "col"), P(("row", "col"), None)),
        out_specs=P(("row", "col"), None),
        check_vma=False,
    )
```
